32 devices in a mesh: dp: 4 (over y, x), tensor: 8 (over z, core).
Axes of the slice: x: 2, y: 2, z: 4, core: 2. Of those that a mesh axis runs over, the one named last changes fastest.
Arguments:
- tokens: bfloat16 [512, 3072], P(('dp', 'tensor')), may hold values from -6 to 6
- tangent_in: bfloat16 [512, 3072], P(('dp', 'tensor')), may hold values from -6 to 6
- cotangent: bfloat16 [512, 3072], P(('dp', 'tensor')), may hold values from -6 to 6
- w_in: bfloat16 [3072, 12288], P('dp', 'tensor'), may hold values from -0.109375 to 0.109375
- w_out: bfloat16 [12288, 3072], P('tensor', 'dp'), may hold values from -0.0546875 to 0.0546875
- clip_len: int32 [16], replicated, may hold values from 1 to 56, as said below
- clip_dev: int32 [16], replicated, may hold values from 0 to 3, as said below
Outputs:
- block_out: bfloat16 [512, 3072], P(('dp', 'tensor'))
- tangent_out: bfloat16 [512, 3072], P(('dp', 'tensor'))
- grad_w_in: float32 [3072, 12288], P('dp', 'tensor')
The draws below stay inside these ranges and needn't reach their ends.
Inputs may be any that keep to these rules, and one draw needn't show every extreme that they name: `clip_len`: the clips of each index of dp have lengths that sum to at most 128; one index reaches 128 in every draw. `clip_dev`: each index of dp holds exactly 4 clips.
All inputs are finite; a program needn't handle non-finite values.
Results may differ from the reference program's by a relative error of at most 0.014.
Values may be sent and summed in bfloat16 or wider, within the bound.
A program may use at most 128 MiB of HBM per device.

```python
import math
import jax
import jax.numpy as jnp
from jax import lax

D = 3072
FF = 12288
ROWS = 128
CLIP_DEV = 4
CLIPS = 16
TOKENS = 512
N_DP = 4
N_TENSOR = 8


def assign_clips(key):
    owners = jnp.arange(CLIPS, dtype=jnp.int32) // CLIP_DEV
    shuffle = jax.random.permutation(key, CLIPS)
    return owners[shuffle]


def draw_clip_dev(key, part):
    return assign_clips(key)


def draw_clip_len(key, part):
    owners = assign_clips(key)
    key = jax.random.fold_in(key, 7)
    key_busy, key_small, key_shift = jax.random.split(key, 3)
    busiest = jax.random.randint(key_busy, (), 0, N_DP, dtype=jnp.int32)
    small_len = jax.random.randint(key_small, (CLIPS,), 1, ROWS // 7, dtype=jnp.int32)
    is_big = owners == busiest
    rank_big = jnp.cumsum(is_big.astype(jnp.int32)) - 1
    widest = ROWS // 4 - ROWS // 16
    other_shift = jax.random.randint(key_shift, (), 0, widest, dtype=jnp.int32)
    base_len = ROWS // CLIP_DEV
    sign_pick = jnp.where(rank_big % 2 == 0, 1, -1)
    shift_pick = jnp.where(rank_big // 2 == 0, widest, other_shift)
    big_len = base_len + sign_pick * shift_pick
    return jnp.where(is_big, big_len, small_len).astype(jnp.int32)


def block_levels(key, dims, cuts, low, largest):
    level = 1.0
    for axis_at, parts in cuts:
        draws = jax.random.uniform(jax.random.fold_in(jax.random.fold_in(key, 6), axis_at), (parts,), jnp.float32, low / len(cuts), largest / len(cuts))
        level = level * jnp.repeat(jnp.exp(draws), dims[axis_at] // parts).reshape((-1,) + (1,) * (len(dims) - 1 - axis_at))
    return level


def noise(rng, dims, deviation, limit, pieces=(), held_as=jnp.bfloat16):
    values = deviation * jax.random.normal(rng, dims, jnp.float32)
    if pieces:
        values = values * block_levels(rng, dims, pieces, -0.22, 0.18)
    return jnp.clip(values, -limit, limit).astype(held_as)


def setup_inputs(seed: int = 0) -> dict:
    streams_of = jax.random.split(jax.random.key(seed), 8)
    tokens = noise(streams_of[0], (TOKENS, D), 1.0, 6.0, ((0, 32),))
    tangent_in = noise(streams_of[1], (TOKENS, D), 1.0, 6.0, ((0, 32),))
    cotangent = noise(streams_of[2], (TOKENS, D), 1.0, 6.0, ((0, 32),))
    w_in = noise(streams_of[3], (D, FF), D ** -0.5, 0.109375, ((0, 4), (1, 8)))
    w_out = noise(streams_of[4], (FF, D), FF ** -0.5, 0.0546875, ((0, 8), (1, 4)))
    clip_len = draw_clip_len(jax.random.fold_in(streams_of[7], 71), 0)
    clip_dev = draw_clip_dev(jax.random.fold_in(streams_of[7], 71), 0)
    return {"tokens": tokens, "tangent_in": tangent_in, "cotangent": cotangent, "w_in": w_in, "w_out": w_out, "clip_len": clip_len, "clip_dev": clip_dev}


tanh_coef = math.sqrt(2.0 / math.pi)
cubic_coef = 0.044715

def gelu_pair(pre_act):
    inner_arg = tanh_coef * (pre_act + cubic_coef * pre_act * pre_act * pre_act)
    tanh_val = jnp.tanh(inner_arg)
    act_val = 0.5 * pre_act * (1.0 + tanh_val)
    slope_val = 0.5 * (1.0 + tanh_val) + 0.5 * pre_act * (1.0 - tanh_val * tanh_val) * tanh_coef * (1.0 + 3.0 * cubic_coef * pre_act * pre_act)
    return (act_val, slope_val)

def reference(tokens, tangent_in, cotangent, w_in, w_out, clip_len, clip_dev):
    owners = jnp.arange(N_DP, dtype=jnp.int32)
    row_loads = lax.optimization_barrier(jnp.sum(jnp.where(clip_dev[None, :] == owners[:, None], clip_len[None, :], 0), axis=1))
    live_mask = (jnp.arange(ROWS, dtype=jnp.int32)[None, :] < row_loads[:, None]).reshape(TOKENS, 1)
    pre_act = jnp.dot(tokens, w_in, preferred_element_type=jnp.float32)
    pre_tan = jnp.dot(tangent_in, w_in, preferred_element_type=jnp.float32)
    act_val, slope_val = gelu_pair(pre_act)
    act_half = act_val.astype(jnp.bfloat16)
    dact_half = (slope_val * pre_tan).astype(jnp.bfloat16)
    hidden_cols = FF // N_TENSOR

    def add_group(running_sums, group_idx):
        col_start = (group_idx * hidden_cols).astype(jnp.int32)
        down_cols = lax.dynamic_slice_in_dim(w_out, col_start, hidden_cols, 0)
        act_cols = lax.dynamic_slice_in_dim(act_half, col_start, hidden_cols, 1)
        dact_cols = lax.dynamic_slice_in_dim(dact_half, col_start, hidden_cols, 1)
        out_term = jnp.where(live_mask, jnp.dot(act_cols, down_cols, preferred_element_type=jnp.float32), 0.0).astype(jnp.bfloat16)
        tan_term = jnp.where(live_mask, jnp.dot(dact_cols, down_cols, preferred_element_type=jnp.float32), 0.0).astype(jnp.bfloat16)
        out_term, tan_term = lax.optimization_barrier((out_term, tan_term))
        return ((running_sums[0] + out_term.astype(jnp.float32), running_sums[1] + tan_term.astype(jnp.float32)), None)
    zero_sum = jnp.zeros((TOKENS, D), jnp.float32)
    (out_sum, tan_sum), _ = lax.scan(add_group, (zero_sum, zero_sum), jnp.arange(N_TENSOR, dtype=jnp.int32))
    back_grad = jnp.dot(cotangent, w_out.T, preferred_element_type=jnp.float32)
    grad_pre = jnp.where(live_mask, slope_val * back_grad, 0.0).astype(jnp.bfloat16)

    def add_rows(running, group_idx):
        row_start = (group_idx * ROWS).astype(jnp.int32)
        tok_rows = lax.dynamic_slice_in_dim(tokens, row_start, ROWS, 0)
        grad_rows = lax.dynamic_slice_in_dim(grad_pre, row_start, ROWS, 0)
        grad_part = lax.dot_general(tok_rows, grad_rows, (((0,), (0,)), ((), ())), preferred_element_type=jnp.float32).astype(jnp.bfloat16)
        grad_part = lax.optimization_barrier(grad_part)
        return (running + grad_part.astype(jnp.float32), None)
    grad_w_in, _ = lax.scan(add_rows, jnp.zeros((D, FF), jnp.float32), jnp.arange(N_DP, dtype=jnp.int32))
    return (out_sum.astype(jnp.bfloat16), tan_sum.astype(jnp.bfloat16), grad_w_in)
```

```python
import math

import jax
import jax.numpy as jnp
from jax import lax
from jax.sharding import PartitionSpec as P

tanh_coef = math.sqrt(2.0 / math.pi)
cubic_coef = 0.044715


def gelu_pair(pre_act):
    inner_arg = tanh_coef * (pre_act + cubic_coef * pre_act * pre_act * pre_act)
    tanh_val = jnp.tanh(inner_arg)
    act_val = 0.5 * pre_act * (1.0 + tanh_val)
    slope_val = 0.5 * (1.0 + tanh_val) + 0.5 * pre_act * (1.0 - tanh_val * tanh_val) * tanh_coef * (
        1.0 + 3.0 * cubic_coef * pre_act * pre_act
    )
    return (act_val, slope_val)


def shift(value, dp_count, step):
    if step % dp_count == 0:
        return value
    return lax.ppermute(value, "dp", [(i, (i + step) % dp_count) for i in range(dp_count)])


def dot(a, b):
    return jnp.dot(a, b, preferred_element_type=jnp.float32)


def local(tokens, tangent_in, cotangent, w_in, w_out, clip_len, clip_dev):
    dp_count = lax.axis_size("dp")
    me = lax.axis_index("dp")
    live_rows = jnp.sum(jnp.where(clip_dev == me, clip_len, 0))
    own_rows, model_cols = tokens.shape
    own_cols = model_cols // dp_count
    steps = range(dp_count)

    rows = jnp.stack([tokens, tangent_in, cotangent]).reshape(3, own_rows, dp_count, own_cols)
    pieces = [
        shift(
            lax.dynamic_index_in_dim(rows, (me + s) % dp_count, 2, keepdims=False), dp_count, s
        )
        for s in steps
    ]
    whole = lax.all_gather(jnp.stack(pieces), "tensor", axis=2, tiled=True)
    group_rows = whole.shape[2]

    f32_own = None
    arrived = []
    for s in list(steps)[1:] + [0]:
        part = [dot(whole[s, 0], w_in), dot(whole[s, 1], w_in)]
        part.append(
            lax.dot_general(
                whole[s, 2], w_out, (((1,), (1,)), ((), ())), preferred_element_type=jnp.float32
            )
        )
        if s == 0:
            f32_own = part
        else:
            arrived.append(shift(jnp.stack([p.astype(jnp.bfloat16) for p in part]), dp_count, -s))
    sums = list(f32_own)
    for piece in arrived:
        sums = [total + piece[k].astype(jnp.float32) for k, total in enumerate(sums)]
    pre_act, pre_tan, back_grad = sums
    keep_row = (jnp.arange(group_rows, dtype=jnp.int32) < live_rows)[:, None]
    act_val, slope_val = gelu_pair(pre_act)
    hidden = jnp.stack(
        [
            jnp.where(keep_row, val, 0.0).astype(jnp.bfloat16)
            for val in (act_val, slope_val * pre_tan, slope_val * back_grad)
        ]
    )

    gathered = [shift(hidden, dp_count, s) for s in steps]
    outs = []
    for s in steps:
        outs.append(
            jnp.stack([dot(gathered[s][k], w_out).astype(jnp.bfloat16) for k in range(2)])
        )
    summed = lax.psum_scatter(jnp.stack(outs), "tensor", scatter_dimension=2, tiled=True)
    cols = jnp.stack([shift(summed[s], dp_count, -s) for s in steps])
    cols = jnp.roll(cols, me, axis=0)
    out, tan = [
        cols[:, k].transpose(1, 0, 2).reshape(own_rows, model_cols) for k in range(2)
    ]
    grad_w_in = lax.dot_general(
        jnp.concatenate([whole[s, 0] for s in steps]),
        jnp.concatenate([gathered[s][2] for s in steps]),
        (((0,), (0,)), ((), ())),
        preferred_element_type=jnp.float32,
    )
    return (out, tan, grad_w_in)


def solution(mesh):
    return jax.shard_map(
        local,
        mesh=mesh,
        in_specs=(
            P(("dp", "tensor"), None),
            P(("dp", "tensor"), None),
            P(("dp", "tensor"), None),
            P("dp", "tensor"),
            P("tensor", "dp"),
            P(),
            P(),
        ),
        out_specs=(P(("dp", "tensor"), None), P(("dp", "tensor"), None), P("dp", "tensor")),
        check_vma=False,
    )
```

```python
import math

import jax
import jax.numpy as jnp
from jax import lax
from jax.sharding import PartitionSpec as P

tanh_coef = math.sqrt(2.0 / math.pi)
cubic_coef = 0.044715


def gelu_pair(pre_act):
    inner_arg = tanh_coef * (pre_act + cubic_coef * pre_act * pre_act * pre_act)
    tanh_val = jnp.tanh(inner_arg)
    act_val = 0.5 * pre_act * (1.0 + tanh_val)
    slope_val = 0.5 * (1.0 + tanh_val) + 0.5 * pre_act * (1.0 - tanh_val * tanh_val) * tanh_coef * (
        1.0 + 3.0 * cubic_coef * pre_act * pre_act
    )
    return (act_val, slope_val)


def dot(a, b):
    return jnp.dot(a, b, preferred_element_type=jnp.float32)


def dp_grid(dp_count):
    lo = int(math.sqrt(dp_count))
    while dp_count % lo:
        lo -= 1
    return dp_count // lo, lo


def shift(value, grid, step):
    hi, lo = grid
    if step[0] % hi == 0 and step[1] % lo == 0:
        return value
    pairs = [
        (a * lo + b, (a + step[0]) % hi * lo + (b + step[1]) % lo)
        for a in range(hi)
        for b in range(lo)
    ]
    return lax.ppermute(value, "dp", pairs)


def axis_step(axis, size):
    return (size, 0) if axis == 0 else (0, size)


def half(value):
    return value.astype(jnp.bfloat16)


def sum_to_owner(part, grid, first):
    second = 1 - first
    n1, n2 = grid[first], grid[second]

    def slot(i, j):
        return (i, j) if first == 0 else (j, i)

    arrived = [
        shift(
            half(jnp.stack([part(slot(i, j)) for j in range(n2)])), grid, axis_step(first, -i)
        )
        for i in range(1, n1)
    ]
    sums = []
    for j in list(range(1, n2)) + [0]:
        total = part(slot(0, j))
        for piece in arrived:
            total = total + piece[j].astype(jnp.float32)
        sums.append(total if j == 0 else shift(half(total), grid, axis_step(second, -j)))
    total = sums[-1]
    for piece in sums[:-1]:
        total = total + piece.astype(jnp.float32)
    return total


def gather_groups(value, grid, first):
    second = 1 - first
    n1, n2 = grid[first], grid[second]
    held = jnp.stack([shift(value, grid, axis_step(first, i)) for i in range(n1)])
    found = {}
    for j in range(n2):
        there = shift(held, grid, axis_step(second, j))
        for i in range(n1):
            found[(i, j) if first == 0 else (j, i)] = there[i]
    return found


def local(tokens, tangent_in, cotangent, w_in, w_out, clip_len, clip_dev):
    dp_count = lax.axis_size("dp")
    grid = dp_grid(dp_count)
    me = lax.axis_index("dp")
    me_hi, me_lo = me // grid[1], me % grid[1]
    live_rows = jnp.sum(jnp.where(clip_dev == me, clip_len, 0))
    own_rows, model_cols = tokens.shape
    own_cols = model_cols // dp_count
    slots = [(i, j) for i in range(grid[0]) for j in range(grid[1])]
    place = {s: k for k, s in enumerate(slots)}

    def own_channels(rows):
        rows = rows.reshape(own_rows, dp_count, own_cols)
        pieces = []
        for i, j in slots:
            target = (me_hi + i) % grid[0] * grid[1] + (me_lo + j) % grid[1]
            piece = lax.dynamic_index_in_dim(rows, target, 1, keepdims=False)
            pieces.append(shift(piece, grid, (i, j)))
        return lax.all_gather(jnp.stack(pieces), "tensor", axis=1, tiled=True)

    tok_cols, tan_cols, cot_cols = [own_channels(v) for v in (tokens, tangent_in, cotangent)]
    group_rows = tok_cols.shape[1]
    cut = group_rows // 2
    halves = [(0, slice(0, cut)), (1, slice(cut, group_rows))]

    def up(cols):
        return [
            sum_to_owner(lambda s, r=rows: dot(cols[place[s], r], w_in), grid, first)
            for first, rows in halves
        ]

    def back(cols):
        return [
            sum_to_owner(
                lambda s, r=rows: lax.dot_general(
                    cols[place[s], r],
                    w_out,
                    (((1,), (1,)), ((), ())),
                    preferred_element_type=jnp.float32,
                ),
                grid,
                first,
            )
            for first, rows in halves
        ]

    row_at = jnp.arange(group_rows, dtype=jnp.int32)
    keep = [(row_at[rows] < live_rows)[:, None] for _, rows in halves]

    def everywhere(values):
        values = [half(jnp.where(k, v, 0.0)) for k, v in zip(keep, values)]
        found = [gather_groups(v, grid, 1 - first) for v, (first, _) in zip(values, halves)]
        return jnp.stack([jnp.concatenate([f[s] for f in found]) for s in slots])

    def down(hidden):
        flat = hidden.reshape(dp_count * group_rows, -1)
        terms = half(dot(flat, w_out)).reshape(dp_count, group_rows, own_cols)
        summed = lax.psum_scatter(terms, "tensor", scatter_dimension=1, tiled=True)
        cols = jnp.stack(
            [shift(summed[place[(i, j)]], grid, (-i, -j)) for i, j in slots]
        ).reshape(*grid, own_rows, own_cols)
        cols = jnp.roll(jnp.roll(cols, me_hi, axis=0), me_lo, axis=1)
        return cols.transpose(2, 0, 1, 3).reshape(own_rows, model_cols)

    pre_act = up(tok_cols)
    pairs = [gelu_pair(p) for p in pre_act]
    act_all = everywhere([a for a, _ in pairs])
    pre_tan = up(tan_cols)
    dact_all = everywhere([s * t for (_, s), t in zip(pairs, pre_tan)])
    back_grad = back(cot_cols)
    grad_all = everywhere([s * g for (_, s), g in zip(pairs, back_grad)])
    out = down(act_all)
    tan = down(dact_all)
    grad_w_in = lax.dot_general(
        tok_cols.reshape(dp_count * group_rows, own_cols),
        grad_all.reshape(dp_count * group_rows, -1),
        (((0,), (0,)), ((), ())),
        preferred_element_type=jnp.float32,
    )
    return (out, tan, grad_w_in)


def solution(mesh):
    return jax.shard_map(
        local,
        mesh=mesh,
        in_specs=(
            P(("dp", "tensor"), None),
            P(("dp", "tensor"), None),
            P(("dp", "tensor"), None),
            P("dp", "tensor"),
            P("tensor", "dp"),
            P(),
            P(),
        ),
        out_specs=(P(("dp", "tensor"), None), P(("dp", "tensor"), None), P("dp", "tensor")),
        check_vma=False,
    )
```

```python
import math

import jax
import jax.numpy as jnp
from jax import lax
from jax.sharding import PartitionSpec as P

tanh_coef = math.sqrt(2.0 / math.pi)
cubic_coef = 0.044715


def gelu_pair(pre_act):
    inner_arg = tanh_coef * (pre_act + cubic_coef * pre_act * pre_act * pre_act)
    tanh_val = jnp.tanh(inner_arg)
    act_val = 0.5 * pre_act * (1.0 + tanh_val)
    slope_val = 0.5 * (1.0 + tanh_val) + 0.5 * pre_act * (1.0 - tanh_val * tanh_val) * tanh_coef * (
        1.0 + 3.0 * cubic_coef * pre_act * pre_act
    )
    return (act_val, slope_val)


def dot(a, b):
    return jnp.dot(a, b, preferred_element_type=jnp.float32)


def dp_grid(dp_count):
    lo = int(math.sqrt(dp_count))
    while dp_count % lo:
        lo -= 1
    return dp_count // lo, lo


def shift(value, grid, step, axis="dp"):
    hi, lo = grid
    if step[0] % hi == 0 and step[1] % lo == 0:
        return value
    pairs = [
        (a * lo + b, (a + step[0]) % hi * lo + (b + step[1]) % lo)
        for a in range(hi)
        for b in range(lo)
    ]
    return lax.ppermute(value, axis, pairs)


def axis_step(axis, size):
    return (size, 0) if axis == 0 else (0, size)


def half(value):
    return value.astype(jnp.bfloat16)


def sum_to_owner(part, grid, first):
    second = 1 - first
    n1, n2 = grid[first], grid[second]

    def slot(i, j):
        return (i, j) if first == 0 else (j, i)

    arrived = [
        shift(
            half(jnp.stack([part(slot(i, j)) for j in range(n2)])), grid, axis_step(first, -i)
        )
        for i in range(1, n1)
    ]
    sums = []
    for j in list(range(1, n2)) + [0]:
        total = part(slot(0, j))
        for piece in arrived:
            total = total + piece[j].astype(jnp.float32)
        sums.append(total if j == 0 else shift(half(total), grid, axis_step(second, -j)))
    total = sums[-1]
    for piece in sums[:-1]:
        total = total + piece.astype(jnp.float32)
    return total


def gather_groups(value, grid, first):
    second = 1 - first
    n1, n2 = grid[first], grid[second]
    held = jnp.stack([shift(value, grid, axis_step(first, i)) for i in range(n1)])
    found = {}
    for j in range(n2):
        there = shift(held, grid, axis_step(second, j))
        for i in range(n1):
            found[(i, j) if first == 0 else (j, i)] = there[i]
    return found


def local(tokens, tangent_in, cotangent, w_in, w_out, clip_len, clip_dev):
    dp_count = lax.axis_size("dp")
    grid = dp_grid(dp_count)
    me = lax.axis_index("dp")
    me_hi, me_lo = me // grid[1], me % grid[1]
    live_rows = jnp.sum(jnp.where(clip_dev == me, clip_len, 0))
    own_rows, model_cols = tokens.shape
    own_cols = model_cols // dp_count
    slots = [(i, j) for i in range(grid[0]) for j in range(grid[1])]
    place = {s: k for k, s in enumerate(slots)}

    tensor_count = lax.axis_size("tensor")
    cores = 2 - tensor_count % 2
    pod = (tensor_count // cores, cores)
    at = lax.axis_index("tensor")
    at_hi, at_lo = at // cores, at % cores

    def own_channels(arrays):
        count = len(arrays)
        pieces = []
        for i, j in slots:
            target = (me_hi + i) % grid[0] * grid[1] + (me_lo + j) % grid[1]
            piece = jnp.stack(
                [lax.dynamic_slice_in_dim(v, target * own_cols, own_cols, 1) for v in arrays]
            )
            pieces.append(shift(piece, grid, (i, j)))
        block = jnp.stack(pieces, axis=1)
        held = jnp.stack([shift(block, pod, (i, 0), "tensor") for i in range(pod[0])], axis=2)
        both = jnp.stack([shift(held, pod, (0, k), "tensor") for k in range(pod[1])], axis=3)
        return both.reshape(count, dp_count, tensor_count * own_rows, own_cols)

    (tok_cols,) = own_channels([tokens])
    tan_cols, cot_cols = own_channels([tangent_in, cotangent])
    group_rows = tok_cols.shape[1]
    cut = group_rows // 2
    halves = [(0, slice(0, cut)), (1, slice(cut, group_rows))]

    def up(cols):
        return [
            sum_to_owner(lambda s, r=rows: dot(cols[place[s], r], w_in), grid, first)
            for first, rows in halves
        ]

    def back(cols):
        return [
            sum_to_owner(
                lambda s, r=rows: lax.dot_general(
                    cols[place[s], r],
                    w_out,
                    (((1,), (1,)), ((), ())),
                    preferred_element_type=jnp.float32,
                ),
                grid,
                first,
            )
            for first, rows in halves
        ]

    back_hi = (at_hi - jnp.arange(pod[0], dtype=jnp.int32)) % pod[0]
    back_lo = (at_lo - jnp.arange(pod[1], dtype=jnp.int32)) % pod[1]
    row_at = (
        (back_hi[:, None] * cores + back_lo[None, :])[:, :, None] * own_rows
        + jnp.arange(own_rows, dtype=jnp.int32)
    ).reshape(group_rows)
    keep = [(row_at[rows] < live_rows)[:, None] for _, rows in halves]

    def everywhere(values):
        values = [half(jnp.where(k, v, 0.0)) for k, v in zip(keep, values)]
        found = [gather_groups(v, grid, 1 - first) for v, (first, _) in zip(values, halves)]
        return jnp.stack([jnp.concatenate([f[s] for f in found]) for s in slots])

    def down(hidden):
        flat = hidden.reshape(dp_count * group_rows, -1)
        terms = dot(flat, w_out).reshape(dp_count, *pod, own_rows, own_cols)
        near = terms[:, :, 0]
        for k in range(1, pod[1]):
            near = near + shift(half(terms[:, :, k]), pod, (0, -k), "tensor").astype(jnp.float32)
        total = near[:, 0]
        for i in range(1, pod[0]):
            total = total + shift(half(near[:, i]), pod, (-i, 0), "tensor").astype(jnp.float32)
        summed = half(total)
        cols = jnp.stack(
            [shift(summed[place[(i, j)]], grid, (-i, -j)) for i, j in slots]
        ).reshape(*grid, own_rows, own_cols)
        cols = jnp.roll(jnp.roll(cols, me_hi, axis=0), me_lo, axis=1)
        return cols.transpose(2, 0, 1, 3).reshape(own_rows, model_cols)

    pre_act = up(tok_cols)
    pairs = [gelu_pair(p) for p in pre_act]
    act_all = everywhere([a for a, _ in pairs])
    pre_tan = up(tan_cols)
    dact_all = everywhere([s * t for (_, s), t in zip(pairs, pre_tan)])
    back_grad = back(cot_cols)
    grad_all = everywhere([s * g for (_, s), g in zip(pairs, back_grad)])
    out = down(act_all)
    tan = down(dact_all)
    grad_w_in = lax.dot_general(
        tok_cols.reshape(dp_count * group_rows, own_cols),
        grad_all.reshape(dp_count * group_rows, -1),
        (((0,), (0,)), ((), ())),
        preferred_element_type=jnp.float32,
    )
    return (out, tan, grad_w_in)


def solution(mesh):
    return jax.shard_map(
        local,
        mesh=mesh,
        in_specs=(
            P(("dp", "tensor"), None),
            P(("dp", "tensor"), None),
            P(("dp", "tensor"), None),
            P("dp", "tensor"),
            P("tensor", "dp"),
            P(),
            P(),
        ),
        out_specs=(P(("dp", "tensor"), None), P(("dp", "tensor"), None), P("dp", "tensor")),
        check_vma=False,
    )
```

```python
import math

import jax
import jax.numpy as jnp
from jax import lax
from jax.sharding import PartitionSpec as P

tanh_coef = math.sqrt(2.0 / math.pi)
cubic_coef = 0.044715


def gelu_pair(pre_act):
    inner_arg = tanh_coef * (pre_act + cubic_coef * pre_act * pre_act * pre_act)
    tanh_val = jnp.tanh(inner_arg)
    act_val = 0.5 * pre_act * (1.0 + tanh_val)
    slope_val = 0.5 * (1.0 + tanh_val) + 0.5 * pre_act * (1.0 - tanh_val * tanh_val) * tanh_coef * (
        1.0 + 3.0 * cubic_coef * pre_act * pre_act
    )
    return (act_val, slope_val)


def dot(a, b):
    return jnp.dot(a, b, preferred_element_type=jnp.float32)


def dp_grid(dp_count):
    lo = int(math.sqrt(dp_count))
    while dp_count % lo:
        lo -= 1
    return dp_count // lo, lo


def shift(value, grid, step, axis="dp"):
    hi, lo = grid
    if step[0] % hi == 0 and step[1] % lo == 0:
        return value
    pairs = [
        (a * lo + b, (a + step[0]) % hi * lo + (b + step[1]) % lo)
        for a in range(hi)
        for b in range(lo)
    ]
    return lax.ppermute(value, axis, pairs)


def axis_step(axis, size):
    return (size, 0) if axis == 0 else (0, size)


def half(value):
    return value.astype(jnp.bfloat16)


def sum_to_owner(part, grid, first):
    second = 1 - first
    n1, n2 = grid[first], grid[second]

    def slot(i, j):
        return (i, j) if first == 0 else (j, i)

    arrived = [
        shift(
            half(jnp.stack([part(slot(i, j)) for j in range(n2)])), grid, axis_step(first, -i)
        )
        for i in range(1, n1)
    ]
    sums = []
    for j in list(range(1, n2)) + [0]:
        total = part(slot(0, j))
        for piece in arrived:
            total = total + piece[j].astype(jnp.float32)
        sums.append(total if j == 0 else shift(half(total), grid, axis_step(second, -j)))
    total = sums[-1]
    for piece in sums[:-1]:
        total = total + piece.astype(jnp.float32)
    return total


def gather_groups(value, grid, first):
    second = 1 - first
    n1, n2 = grid[first], grid[second]
    held = jnp.stack([shift(value, grid, axis_step(first, i)) for i in range(n1)])
    found = {}
    for j in range(n2):
        there = shift(held, grid, axis_step(second, j))
        for i in range(n1):
            found[(i, j) if first == 0 else (j, i)] = there[i]
    return found


def local(tokens, tangent_in, cotangent, w_in, w_out, clip_len, clip_dev):
    dp_count = lax.axis_size("dp")
    grid = dp_grid(dp_count)
    me = lax.axis_index("dp")
    me_hi, me_lo = me // grid[1], me % grid[1]
    live_rows = jnp.sum(jnp.where(clip_dev == me, clip_len, 0))
    own_rows, model_cols = tokens.shape
    own_cols = model_cols // dp_count
    slots = [(i, j) for i in range(grid[0]) for j in range(grid[1])]
    place = {s: k for k, s in enumerate(slots)}

    tensor_count = lax.axis_size("tensor")
    cores = 2 - tensor_count % 2
    pod = (tensor_count // cores, cores)
    at = lax.axis_index("tensor")
    at_hi, at_lo = at // cores, at % cores

    pieces = []
    for i, j in slots:
        target = (me_hi + i) % grid[0] * grid[1] + (me_lo + j) % grid[1]
        piece = jnp.stack(
            [
                lax.dynamic_slice_in_dim(v, target * own_cols, own_cols, 1)
                for v in (tokens, tangent_in, cotangent)
            ]
        )
        pieces.append(shift(piece, grid, (i, j)))

    def own_channels(block):
        held = jnp.stack([shift(block, pod, (i, 0), "tensor") for i in range(pod[0])], axis=2)
        both = jnp.stack([shift(held, pod, (0, k), "tensor") for k in range(pod[1])], axis=3)
        return both.reshape(-1, dp_count, tensor_count * own_rows, own_cols)

    (tok_cols,) = own_channels(jnp.stack([p[:1] for p in pieces], axis=1))
    later = jnp.stack([p[1:] for p in pieces], axis=1)
    later, _ = lax.optimization_barrier((later, tok_cols))
    tan_cols, cot_cols = own_channels(later)
    group_rows = tok_cols.shape[1]
    cut = group_rows // 2
    halves = [(0, slice(0, cut)), (1, slice(cut, group_rows))]

    def up(rows):
        return dot(rows, w_in)

    def back(rows):
        return lax.dot_general(
            rows, w_out, (((1,), (1,)), ((), ())), preferred_element_type=jnp.float32
        )

    def sums(terms):
        return [
            sum_to_owner(
                lambda s, r=rows: jnp.stack([f(cols[place[s], r]) for f, cols in terms]),
                grid,
                first,
            )
            for first, rows in halves
        ]

    back_hi = (at_hi - jnp.arange(pod[0], dtype=jnp.int32)) % pod[0]
    back_lo = (at_lo - jnp.arange(pod[1], dtype=jnp.int32)) % pod[1]
    row_at = (
        (back_hi[:, None] * cores + back_lo[None, :])[:, :, None] * own_rows
        + jnp.arange(own_rows, dtype=jnp.int32)
    ).reshape(group_rows)
    keep = [(row_at[rows] < live_rows)[:, None] for _, rows in halves]

    def everywhere(values):
        values = [half(jnp.where(k, v, 0.0)) for k, v in zip(keep, values)]
        found = [gather_groups(v, grid, 1 - first) for v, (first, _) in zip(values, halves)]
        return jnp.stack([jnp.concatenate([f[s] for f in found]) for s in slots])

    def down(hidden):
        flat = hidden.reshape(dp_count * group_rows, -1)
        terms = dot(flat, w_out).reshape(dp_count, *pod, own_rows, own_cols)
        near = terms[:, :, 0]
        for k in range(1, pod[1]):
            near = near + shift(half(terms[:, :, k]), pod, (0, -k), "tensor").astype(jnp.float32)
        total = near[:, 0]
        for i in range(1, pod[0]):
            total = total + shift(half(near[:, i]), pod, (-i, 0), "tensor").astype(jnp.float32)
        return half(total)

    pre_act = [p[0] for p in sums([(up, tok_cols)])]
    pairs = [gelu_pair(p) for p in pre_act]
    act_all = everywhere([a for a, _ in pairs])
    both = sums([(up, tan_cols), (back, cot_cols)])
    dact_all = everywhere([s * v[0] for (_, s), v in zip(pairs, both)])
    grad_all = everywhere([s * v[1] for (_, s), v in zip(pairs, both)])
    summed = jnp.stack([down(act_all), down(dact_all)], axis=1)
    cols = jnp.stack(
        [shift(summed[place[(i, j)]], grid, (-i, -j)) for i, j in slots]
    ).reshape(*grid, 2, own_rows, own_cols)
    cols = jnp.roll(jnp.roll(cols, me_hi, axis=0), me_lo, axis=1)
    out, tan = cols.transpose(2, 3, 0, 1, 4).reshape(2, own_rows, model_cols)
    grad_w_in = lax.dot_general(
        tok_cols.reshape(dp_count * group_rows, own_cols),
        grad_all.reshape(dp_count * group_rows, -1),
        (((0,), (0,)), ((), ())),
        preferred_element_type=jnp.float32,
    )
    return (out, tan, grad_w_in)


def solution(mesh):
    return jax.shard_map(
        local,
        mesh=mesh,
        in_specs=(
            P(("dp", "tensor"), None),
            P(("dp", "tensor"), None),
            P(("dp", "tensor"), None),
            P("dp", "tensor"),
            P("tensor", "dp"),
            P(),
            P(),
        ),
        out_specs=(P(("dp", "tensor"), None), P(("dp", "tensor"), None), P("dp", "tensor")),
        check_vma=False,
    )
```

```python
import math

import jax
import jax.numpy as jnp
from jax import lax
from jax.sharding import PartitionSpec as P

tanh_coef = math.sqrt(2.0 / math.pi)
cubic_coef = 0.044715


def gelu_pair(pre_act):
    inner_arg = tanh_coef * (pre_act + cubic_coef * pre_act * pre_act * pre_act)
    tanh_val = jnp.tanh(inner_arg)
    act_val = 0.5 * pre_act * (1.0 + tanh_val)
    slope_val = 0.5 * (1.0 + tanh_val) + 0.5 * pre_act * (1.0 - tanh_val * tanh_val) * tanh_coef * (
        1.0 + 3.0 * cubic_coef * pre_act * pre_act
    )
    return (act_val, slope_val)


def dot(a, b):
    return jnp.dot(a, b, preferred_element_type=jnp.float32)


def dp_grid(dp_count):
    lo = int(math.sqrt(dp_count))
    while dp_count % lo:
        lo -= 1
    return dp_count // lo, lo


def shift(value, grid, step, axis="dp"):
    hi, lo = grid
    if step[0] % hi == 0 and step[1] % lo == 0:
        return value
    pairs = [
        (a * lo + b, (a + step[0]) % hi * lo + (b + step[1]) % lo)
        for a in range(hi)
        for b in range(lo)
    ]
    return lax.ppermute(value, axis, pairs)


def after(value, *others):
    return lax.optimization_barrier((value, others))[0]


def axis_step(axis, size):
    return (size, 0) if axis == 0 else (0, size)


def half(value):
    return value.astype(jnp.bfloat16)


def sum_to_owner(part, grid, first):
    second = 1 - first
    n1, n2 = grid[first], grid[second]

    def slot(i, j):
        return (i, j) if first == 0 else (j, i)

    arrived = [
        shift(
            half(jnp.stack([part(slot(i, j)) for j in range(n2)])), grid, axis_step(first, -i)
        )
        for i in range(1, n1)
    ]
    sums = []
    for j in list(range(1, n2)) + [0]:
        total = part(slot(0, j))
        for piece in arrived:
            total = total + piece[j].astype(jnp.float32)
        sums.append(total if j == 0 else shift(half(total), grid, axis_step(second, -j)))
    total = sums[-1]
    for piece in sums[:-1]:
        total = total + piece.astype(jnp.float32)
    return total


def gather_first(value, grid, first):
    return jnp.stack([shift(value, grid, axis_step(first, i)) for i in range(grid[first])])


def gather_second(held, grid, first):
    second = 1 - first
    found = {}
    for j in range(grid[second]):
        there = shift(held, grid, axis_step(second, j))
        for i in range(grid[first]):
            found[(i, j) if first == 0 else (j, i)] = there[i]
    return found


def local(tokens, tangent_in, cotangent, w_in, w_out, clip_len, clip_dev):
    dp_count = lax.axis_size("dp")
    grid = dp_grid(dp_count)
    me = lax.axis_index("dp")
    me_hi, me_lo = me // grid[1], me % grid[1]
    live_rows = jnp.sum(jnp.where(clip_dev == me, clip_len, 0))
    own_rows, model_cols = tokens.shape
    own_cols = model_cols // dp_count
    slots = [(i, j) for i in range(grid[0]) for j in range(grid[1])]
    place = {s: k for k, s in enumerate(slots)}

    tensor_count = lax.axis_size("tensor")
    cores = 2 - tensor_count % 2
    pod = (tensor_count // cores, cores)
    at = lax.axis_index("tensor")
    at_hi, at_lo = at // cores, at % cores

    pieces = []
    for i, j in slots:
        target = (me_hi + i) % grid[0] * grid[1] + (me_lo + j) % grid[1]
        piece = jnp.stack(
            [
                lax.dynamic_slice_in_dim(v, target * own_cols, own_cols, 1)
                for v in (tokens, tangent_in, cotangent)
            ]
        )
        pieces.append(shift(piece, grid, (i, j)))

    def from_chips(block):
        return jnp.stack([shift(block, pod, (i, 0), "tensor") for i in range(pod[0])], axis=2)

    def from_cores(held):
        both = jnp.stack([shift(held, pod, (0, k), "tensor") for k in range(pod[1])], axis=3)
        return both.reshape(-1, dp_count, tensor_count * own_rows, own_cols)

    (tok_cols,) = from_cores(from_chips(jnp.stack([p[:1] for p in pieces], axis=1)))
    later = from_chips(after(jnp.stack([p[1:] for p in pieces], axis=1), tok_cols))
    group_rows = tok_cols.shape[1]
    cut = group_rows // 2
    halves = [(0, slice(0, cut)), (1, slice(cut, group_rows))]

    def up(rows):
        return dot(rows, w_in)

    def back(rows):
        return lax.dot_general(
            rows, w_out, (((1,), (1,)), ((), ())), preferred_element_type=jnp.float32
        )

    def sums(terms):
        return [
            sum_to_owner(
                lambda s, r=rows: jnp.stack([f(cols[place[s], r]) for f, cols in terms]),
                grid,
                first,
            )
            for first, rows in halves
        ]

    back_hi = (at_hi - jnp.arange(pod[0], dtype=jnp.int32)) % pod[0]
    back_lo = (at_lo - jnp.arange(pod[1], dtype=jnp.int32)) % pod[1]
    row_at = (
        (back_hi[:, None] * cores + back_lo[None, :])[:, :, None] * own_rows
        + jnp.arange(own_rows, dtype=jnp.int32)
    ).reshape(group_rows)
    keep = [(row_at[rows] < live_rows)[:, None] for _, rows in halves]

    def spread(values):
        values = [half(jnp.where(k, v, 0.0)) for k, v in zip(keep, values)]
        return [gather_first(v, grid, 1 - first) for v, (first, _) in zip(values, halves)]

    def everywhere(held):
        found = [gather_second(v, grid, 1 - first) for v, (first, _) in zip(held, halves)]
        return jnp.stack([jnp.concatenate([f[s] for f in found]) for s in slots])

    def down_cores(hidden):
        flat = hidden.reshape(dp_count * group_rows, -1)
        terms = dot(flat, w_out).reshape(dp_count, *pod, own_rows, own_cols)
        near = terms[:, :, 0]
        for k in range(1, pod[1]):
            near = near + shift(half(terms[:, :, k]), pod, (0, -k), "tensor").astype(jnp.float32)
        return near

    def down_chips(near):
        total = near[:, 0]
        for i in range(1, pod[0]):
            total = total + shift(half(near[:, i]), pod, (-i, 0), "tensor").astype(jnp.float32)
        return half(total)

    pre_act = [p[0] for p in sums([(up, tok_cols)])]
    pairs = [gelu_pair(p) for p in pre_act]
    act_held = spread([a for a, _ in pairs])
    later = from_cores(after(later, pre_act))
    tan_cols, cot_cols = after(later, act_held)
    act_all = everywhere(act_held)
    both = sums([(up, tan_cols), (back, cot_cols)])
    out_near = down_cores(act_all)
    both = after(both, out_near)
    dact_held = spread([s * v[0] for (_, s), v in zip(pairs, both)])
    dact_all = everywhere(dact_held)
    back_grad = after([v[1] for v in both], dact_held)
    grad_all = everywhere(spread([s * v for (_, s), v in zip(pairs, back_grad)]))
    summed = jnp.stack([down_chips(out_near), down_chips(down_cores(dact_all))], axis=1)
    cols = jnp.stack(
        [shift(summed[place[(i, j)]], grid, (-i, -j)) for i, j in slots]
    ).reshape(*grid, 2, own_rows, own_cols)
    cols = jnp.roll(jnp.roll(cols, me_hi, axis=0), me_lo, axis=1)
    out, tan = cols.transpose(2, 3, 0, 1, 4).reshape(2, own_rows, model_cols)
    grad_w_in = lax.dot_general(
        tok_cols.reshape(dp_count * group_rows, own_cols),
        grad_all.reshape(dp_count * group_rows, -1),
        (((0,), (0,)), ((), ())),
        preferred_element_type=jnp.float32,
    )
    return (out, tan, grad_w_in)


def solution(mesh):
    return jax.shard_map(
        local,
        mesh=mesh,
        in_specs=(
            P(("dp", "tensor"), None),
            P(("dp", "tensor"), None),
            P(("dp", "tensor"), None),
            P("dp", "tensor"),
            P("tensor", "dp"),
            P(),
            P(),
        ),
        out_specs=(P(("dp", "tensor"), None), P(("dp", "tensor"), None), P("dp", "tensor")),
        check_vma=False,
    )
```

```python
import math

import jax
import jax.numpy as jnp
from jax import lax
from jax.sharding import PartitionSpec as P

tanh_coef = math.sqrt(2.0 / math.pi)
cubic_coef = 0.044715


def gelu_pair(pre_act):
    inner_arg = tanh_coef * (pre_act + cubic_coef * pre_act * pre_act * pre_act)
    tanh_val = jnp.tanh(inner_arg)
    act_val = 0.5 * pre_act * (1.0 + tanh_val)
    slope_val = 0.5 * (1.0 + tanh_val) + 0.5 * pre_act * (1.0 - tanh_val * tanh_val) * tanh_coef * (
        1.0 + 3.0 * cubic_coef * pre_act * pre_act
    )
    return (act_val, slope_val)


def dot(a, b):
    return jnp.dot(a, b, preferred_element_type=jnp.float32)


def dp_grid(dp_count):
    lo = int(math.sqrt(dp_count))
    while dp_count % lo:
        lo -= 1
    return dp_count // lo, lo


def shift(value, grid, step, axis="dp"):
    hi, lo = grid
    if step[0] % hi == 0 and step[1] % lo == 0:
        return value
    pairs = [
        (a * lo + b, (a + step[0]) % hi * lo + (b + step[1]) % lo)
        for a in range(hi)
        for b in range(lo)
    ]
    return lax.ppermute(value, axis, pairs)


def after(value, *others):
    return lax.optimization_barrier((value, others))[0]


def axis_step(axis, size):
    return (size, 0) if axis == 0 else (0, size)


def half(value):
    return value.astype(jnp.bfloat16)


def sum_to_owner(part, grid, first):
    second = 1 - first
    n1, n2 = grid[first], grid[second]

    def slot(i, j):
        return (i, j) if first == 0 else (j, i)

    arrived = [
        shift(
            half(jnp.stack([part(slot(i, j)) for j in range(n2)])), grid, axis_step(first, -i)
        )
        for i in range(1, n1)
    ]
    sums = []
    for j in list(range(1, n2)) + [0]:
        total = part(slot(0, j))
        for piece in arrived:
            total = total + piece[j].astype(jnp.float32)
        sums.append(total if j == 0 else shift(half(total), grid, axis_step(second, -j)))
    total = sums[-1]
    for piece in sums[:-1]:
        total = total + piece.astype(jnp.float32)
    return total


def gather_first(value, grid, first):
    return jnp.stack([shift(value, grid, axis_step(first, i)) for i in range(grid[first])])


def gather_second(held, grid, first):
    second = 1 - first
    found = {}
    for j in range(grid[second]):
        there = shift(held, grid, axis_step(second, j))
        for i in range(grid[first]):
            found[(i, j) if first == 0 else (j, i)] = there[i]
    return found


def local(tokens, tangent_in, cotangent, w_in, w_out, clip_len, clip_dev):
    dp_count = lax.axis_size("dp")
    grid = dp_grid(dp_count)
    me = lax.axis_index("dp")
    me_hi, me_lo = me // grid[1], me % grid[1]
    live_rows = jnp.sum(jnp.where(clip_dev == me, clip_len, 0))
    own_rows, model_cols = tokens.shape
    own_cols = model_cols // dp_count
    slots = [(i, j) for i in range(grid[0]) for j in range(grid[1])]
    place = {s: k for k, s in enumerate(slots)}

    tensor_count = lax.axis_size("tensor")
    cores = 2 - tensor_count % 2
    pod = (tensor_count // cores, cores)
    at = lax.axis_index("tensor")
    at_hi, at_lo = at // cores, at % cores

    pieces = []
    for i, j in slots:
        target = (me_hi + i) % grid[0] * grid[1] + (me_lo + j) % grid[1]
        piece = jnp.stack(
            [
                lax.dynamic_slice_in_dim(v, target * own_cols, own_cols, 1)
                for v in (tokens, tangent_in, cotangent)
            ]
        )
        pieces.append(shift(piece, grid, (i, j)))

    def from_chips(block):
        return jnp.stack([shift(block, pod, (i, 0), "tensor") for i in range(pod[0])], axis=2)

    def from_cores(held):
        both = jnp.stack([shift(held, pod, (0, k), "tensor") for k in range(pod[1])], axis=3)
        return both.reshape(-1, dp_count, tensor_count * own_rows, own_cols)

    (tok_cols,) = from_cores(from_chips(jnp.stack([p[:1] for p in pieces], axis=1)))
    later = from_chips(after(jnp.stack([p[1:] for p in pieces], axis=1), tok_cols))
    group_rows = tok_cols.shape[1]
    cut = group_rows // 2
    halves = [(0, slice(0, cut)), (1, slice(cut, group_rows))]

    def up(rows):
        return dot(rows, w_in)

    def back(rows):
        return lax.dot_general(
            rows, w_out, (((1,), (1,)), ((), ())), preferred_element_type=jnp.float32
        )

    def sums(terms):
        return [
            sum_to_owner(
                lambda s, r=rows: jnp.stack([f(cols[place[s], r]) for f, cols in terms]),
                grid,
                first,
            )
            for first, rows in halves
        ]

    back_hi = (at_hi - jnp.arange(pod[0], dtype=jnp.int32)) % pod[0]
    back_lo = (at_lo - jnp.arange(pod[1], dtype=jnp.int32)) % pod[1]
    row_at = (
        (back_hi[:, None] * cores + back_lo[None, :])[:, :, None] * own_rows
        + jnp.arange(own_rows, dtype=jnp.int32)
    ).reshape(group_rows)
    keep = [(row_at[rows] < live_rows)[:, None] for _, rows in halves]

    def spread(values):
        values = [half(jnp.where(k, v, 0.0)) for k, v in zip(keep, values)]
        return [gather_first(v, grid, 1 - first) for v, (first, _) in zip(values, halves)]

    def everywhere(held):
        found = [gather_second(v, grid, 1 - first) for v, (first, _) in zip(held, halves)]
        return jnp.stack([jnp.concatenate([f[s] for f in found]) for s in slots])

    def down_cores(hidden):
        flat = hidden.reshape(dp_count * group_rows, -1)
        terms = dot(flat, w_out).reshape(dp_count, *pod, own_rows, own_cols)
        near = terms[:, :, 0]
        for k in range(1, pod[1]):
            near = near + shift(half(terms[:, :, k]), pod, (0, -k), "tensor").astype(jnp.float32)
        return near

    def down_chips(near):
        total = near[:, 0]
        for i in range(1, pod[0]):
            total = total + shift(half(near[:, i]), pod, (-i, 0), "tensor").astype(jnp.float32)
        return half(total)

    pre_act = [p[0] for p in sums([(up, tok_cols)])]
    pre_act, later = lax.optimization_barrier((pre_act, later))
    pairs = [gelu_pair(p) for p in pre_act]
    act_held = spread([a for a, _ in pairs])
    later = from_cores(later)
    tan_cols, cot_cols = after(later, act_held)
    act_all = everywhere(act_held)
    both = sums([(up, tan_cols), (back, cot_cols)])
    out_near = down_cores(act_all)
    both = after(both, out_near)
    dact_held = spread([s * v[0] for (_, s), v in zip(pairs, both)])
    dact_all = everywhere(dact_held)
    dact_all, back_grad = lax.optimization_barrier((dact_all, [v[1] for v in both]))
    grad_all = everywhere(spread([s * v for (_, s), v in zip(pairs, back_grad)]))
    summed = jnp.stack([down_chips(out_near), down_chips(down_cores(dact_all))], axis=1)
    cols = jnp.stack(
        [shift(summed[place[(i, j)]], grid, (-i, -j)) for i, j in slots]
    ).reshape(*grid, 2, own_rows, own_cols)
    cols = jnp.roll(jnp.roll(cols, me_hi, axis=0), me_lo, axis=1)
    out, tan = cols.transpose(2, 3, 0, 1, 4).reshape(2, own_rows, model_cols)
    grad_w_in = lax.dot_general(
        tok_cols.reshape(dp_count * group_rows, own_cols),
        grad_all.reshape(dp_count * group_rows, -1),
        (((0,), (0,)), ((), ())),
        preferred_element_type=jnp.float32,
    )
    return (out, tan, grad_w_in)


def solution(mesh):
    return jax.shard_map(
        local,
        mesh=mesh,
        in_specs=(
            P(("dp", "tensor"), None),
            P(("dp", "tensor"), None),
            P(("dp", "tensor"), None),
            P("dp", "tensor"),
            P("tensor", "dp"),
            P(),
            P(),
        ),
        out_specs=(P(("dp", "tensor"), None), P(("dp", "tensor"), None), P("dp", "tensor")),
        check_vma=False,
    )
```

```python
import math

import jax
import jax.numpy as jnp
from jax import lax
from jax.sharding import PartitionSpec as P

tanh_coef = math.sqrt(2.0 / math.pi)
cubic_coef = 0.044715


def gelu_pair(pre_act):
    inner_arg = tanh_coef * (pre_act + cubic_coef * pre_act * pre_act * pre_act)
    tanh_val = jnp.tanh(inner_arg)
    act_val = 0.5 * pre_act * (1.0 + tanh_val)
    slope_val = 0.5 * (1.0 + tanh_val) + 0.5 * pre_act * (1.0 - tanh_val * tanh_val) * tanh_coef * (
        1.0 + 3.0 * cubic_coef * pre_act * pre_act
    )
    return (act_val, slope_val)


def dot(a, b):
    return jnp.dot(a, b, preferred_element_type=jnp.float32)


def dp_grid(dp_count):
    lo = int(math.sqrt(dp_count))
    while dp_count % lo:
        lo -= 1
    return dp_count // lo, lo


def shift(value, grid, step, axis="dp"):
    hi, lo = grid
    if step[0] % hi == 0 and step[1] % lo == 0:
        return value
    pairs = [
        (a * lo + b, (a + step[0]) % hi * lo + (b + step[1]) % lo)
        for a in range(hi)
        for b in range(lo)
    ]
    return lax.ppermute(value, axis, pairs)


def after(value, *others):
    return lax.optimization_barrier((value, others))[0]


def axis_step(axis, size):
    return (size, 0) if axis == 0 else (0, size)


def half(value):
    return value.astype(jnp.bfloat16)


def slot_of(i, j, first):
    return (i, j) if first == 0 else (j, i)


def sum_first(part, grid, first):
    n1, n2 = grid[first], grid[1 - first]
    return [
        shift(
            half(jnp.stack([part(slot_of(i, j, first)) for j in range(n2)])),
            grid,
            axis_step(first, -i),
        )
        for i in range(1, n1)
    ]


def sum_second(part, arrived, grid, first):
    second = 1 - first
    n2 = grid[second]
    sums = []
    for j in list(range(1, n2)) + [0]:
        total = part(slot_of(0, j, first))
        for piece in arrived:
            total = total + piece[j].astype(jnp.float32)
        sums.append(total if j == 0 else shift(half(total), grid, axis_step(second, -j)))
    total = sums[-1]
    for piece in sums[:-1]:
        total = total + piece.astype(jnp.float32)
    return total


def gather_first(value, grid, first):
    return jnp.stack([shift(value, grid, axis_step(first, i)) for i in range(grid[first])])


def gather_second(held, grid, first):
    second = 1 - first
    found = {}
    for j in range(grid[second]):
        there = shift(held, grid, axis_step(second, j))
        for i in range(grid[first]):
            found[(i, j) if first == 0 else (j, i)] = there[i]
    return found


def local(tokens, tangent_in, cotangent, w_in, w_out, clip_len, clip_dev):
    dp_count = lax.axis_size("dp")
    grid = dp_grid(dp_count)
    me = lax.axis_index("dp")
    me_hi, me_lo = me // grid[1], me % grid[1]
    live_rows = jnp.sum(jnp.where(clip_dev == me, clip_len, 0))
    own_rows, model_cols = tokens.shape
    own_cols = model_cols // dp_count
    slots = [(i, j) for i in range(grid[0]) for j in range(grid[1])]
    place = {s: k for k, s in enumerate(slots)}

    tensor_count = lax.axis_size("tensor")
    cores = 2 - tensor_count % 2
    pod = (tensor_count // cores, cores)
    at = lax.axis_index("tensor")
    at_hi, at_lo = at // cores, at % cores

    pieces = []
    for i, j in slots:
        target = (me_hi + i) % grid[0] * grid[1] + (me_lo + j) % grid[1]
        piece = jnp.stack(
            [
                lax.dynamic_slice_in_dim(v, target * own_cols, own_cols, 1)
                for v in (tokens, tangent_in, cotangent)
            ]
        )
        pieces.append(shift(piece, grid, (i, j)))

    def from_chips(block):
        return jnp.stack([shift(block, pod, (i, 0), "tensor") for i in range(pod[0])], axis=2)

    def from_cores(held):
        both = jnp.stack([shift(held, pod, (0, k), "tensor") for k in range(pod[1])], axis=3)
        return both.reshape(-1, dp_count, tensor_count * own_rows, own_cols)

    (tok_cols,) = from_cores(from_chips(jnp.stack([p[:1] for p in pieces], axis=1)))
    later = jnp.stack([p[1:] for p in pieces], axis=1)
    group_rows = tok_cols.shape[1]
    cut = group_rows // 2
    halves = [(0, slice(0, cut)), (1, slice(cut, group_rows))]

    def up(rows):
        return dot(rows, w_in)

    def back(rows):
        return lax.dot_general(
            rows, w_out, (((1,), (1,)), ((), ())), preferred_element_type=jnp.float32
        )

    def parts(terms):
        return [
            (lambda s, r=rows: jnp.stack([f(cols[place[s], r]) for f, cols in terms]), grid, first)
            for first, rows in halves
        ]

    def sums_first(terms):
        return [sum_first(*p) for p in parts(terms)]

    def sums_second(terms, arrived):
        return [sum_second(p[0], a, *p[1:]) for p, a in zip(parts(terms), arrived)]

    back_hi = (at_hi - jnp.arange(pod[0], dtype=jnp.int32)) % pod[0]
    back_lo = (at_lo - jnp.arange(pod[1], dtype=jnp.int32)) % pod[1]
    row_at = (
        (back_hi[:, None] * cores + back_lo[None, :])[:, :, None] * own_rows
        + jnp.arange(own_rows, dtype=jnp.int32)
    ).reshape(group_rows)
    keep = [(row_at[rows] < live_rows)[:, None] for _, rows in halves]

    def spread(values):
        values = [half(jnp.where(k, v, 0.0)) for k, v in zip(keep, values)]
        return [gather_first(v, grid, 1 - first) for v, (first, _) in zip(values, halves)]

    def everywhere(held):
        found = [gather_second(v, grid, 1 - first) for v, (first, _) in zip(held, halves)]
        return jnp.stack([jnp.concatenate([f[s] for f in found]) for s in slots])

    def down_cores(hidden):
        flat = hidden.reshape(dp_count * group_rows, -1)
        terms = dot(flat, w_out).reshape(dp_count, *pod, own_rows, own_cols)
        near = terms[:, :, 0]
        for k in range(1, pod[1]):
            near = near + shift(half(terms[:, :, k]), pod, (0, -k), "tensor").astype(jnp.float32)
        return near

    def down_chips(near):
        total = near[:, 0]
        for i in range(1, pod[0]):
            total = total + shift(half(near[:, i]), pod, (-i, 0), "tensor").astype(jnp.float32)
        return half(total)

    arrived = sums_first([(up, tok_cols)])
    arrived, later = lax.optimization_barrier((arrived, later))
    later = from_chips(later)
    pre_act = [p[0] for p in sums_second([(up, tok_cols)], arrived)]
    pairs = [gelu_pair(p) for p in pre_act]
    act_held = spread([a for a, _ in pairs])
    later = from_cores(after(later, pre_act))
    tan_cols, cot_cols = after(later, act_held)
    act_all = everywhere(act_held)
    terms = [(up, tan_cols), (back, cot_cols)]
    both = sums_second(terms, sums_first(terms))
    out_near = down_cores(act_all)
    both = after(both, out_near)
    dact_held = spread([s * v[0] for (_, s), v in zip(pairs, both)])
    dact_all = everywhere(dact_held)
    back_grad = after([v[1] for v in both], dact_held)
    grad_held = spread([s * v for (_, s), v in zip(pairs, back_grad)])
    dact_all, grad_held = lax.optimization_barrier((dact_all, grad_held))
    grad_all = everywhere(grad_held)
    summed = jnp.stack([down_chips(out_near), down_chips(down_cores(dact_all))], axis=1)
    cols = jnp.stack(
        [shift(summed[place[(i, j)]], grid, (-i, -j)) for i, j in slots]
    ).reshape(*grid, 2, own_rows, own_cols)
    cols = jnp.roll(jnp.roll(cols, me_hi, axis=0), me_lo, axis=1)
    out, tan = cols.transpose(2, 3, 0, 1, 4).reshape(2, own_rows, model_cols)
    grad_w_in = lax.dot_general(
        tok_cols.reshape(dp_count * group_rows, own_cols),
        grad_all.reshape(dp_count * group_rows, -1),
        (((0,), (0,)), ((), ())),
        preferred_element_type=jnp.float32,
    )
    return (out, tan, grad_w_in)


def solution(mesh):
    return jax.shard_map(
        local,
        mesh=mesh,
        in_specs=(
            P(("dp", "tensor"), None),
            P(("dp", "tensor"), None),
            P(("dp", "tensor"), None),
            P("dp", "tensor"),
            P("tensor", "dp"),
            P(),
            P(),
        ),
        out_specs=(P(("dp", "tensor"), None), P(("dp", "tensor"), None), P("dp", "tensor")),
        check_vma=False,
    )
```

```python
import math

import jax
import jax.numpy as jnp
from jax import lax
from jax.sharding import PartitionSpec as P

tanh_coef = math.sqrt(2.0 / math.pi)
cubic_coef = 0.044715


def gelu_pair(pre_act):
    inner_arg = tanh_coef * (pre_act + cubic_coef * pre_act * pre_act * pre_act)
    tanh_val = jnp.tanh(inner_arg)
    act_val = 0.5 * pre_act * (1.0 + tanh_val)
    slope_val = 0.5 * (1.0 + tanh_val) + 0.5 * pre_act * (1.0 - tanh_val * tanh_val) * tanh_coef * (
        1.0 + 3.0 * cubic_coef * pre_act * pre_act
    )
    return (act_val, slope_val)


def dot(a, b):
    return jnp.dot(a, b, preferred_element_type=jnp.float32)


def dp_grid(dp_count):
    lo = int(math.sqrt(dp_count))
    while dp_count % lo:
        lo -= 1
    return dp_count // lo, lo


def shift(value, grid, step, axis="dp"):
    hi, lo = grid
    if step[0] % hi == 0 and step[1] % lo == 0:
        return value
    pairs = [
        (a * lo + b, (a + step[0]) % hi * lo + (b + step[1]) % lo)
        for a in range(hi)
        for b in range(lo)
    ]
    return lax.ppermute(value, axis, pairs)


def after(value, *others):
    return lax.optimization_barrier((value, others))[0]


def axis_step(axis, size):
    return (size, 0) if axis == 0 else (0, size)


def half(value):
    return value.astype(jnp.bfloat16)


def sum_to_owner(part, grid, first):
    second = 1 - first
    n1, n2 = grid[first], grid[second]

    def slot(i, j):
        return (i, j) if first == 0 else (j, i)

    arrived = [
        shift(
            half(jnp.stack([part(slot(i, j)) for j in range(n2)])), grid, axis_step(first, -i)
        )
        for i in range(1, n1)
    ]
    sums = []
    for j in list(range(1, n2)) + [0]:
        total = part(slot(0, j))
        for piece in arrived:
            total = total + piece[j].astype(jnp.float32)
        sums.append(total if j == 0 else shift(half(total), grid, axis_step(second, -j)))
    total = sums[-1]
    for piece in sums[:-1]:
        total = total + piece.astype(jnp.float32)
    return total


def gather_first(value, grid, first):
    return jnp.stack([shift(value, grid, axis_step(first, i)) for i in range(grid[first])])


def gather_second(held, grid, first):
    second = 1 - first
    found = {}
    for j in range(grid[second]):
        there = shift(held, grid, axis_step(second, j))
        for i in range(grid[first]):
            found[(i, j) if first == 0 else (j, i)] = there[i]
    return found


def local(tokens, tangent_in, cotangent, w_in, w_out, clip_len, clip_dev):
    dp_count = lax.axis_size("dp")
    grid = dp_grid(dp_count)
    me = lax.axis_index("dp")
    me_hi, me_lo = me // grid[1], me % grid[1]
    live_rows = jnp.sum(jnp.where(clip_dev == me, clip_len, 0))
    own_rows, model_cols = tokens.shape
    own_cols = model_cols // dp_count
    slots = [(i, j) for i in range(grid[0]) for j in range(grid[1])]
    place = {s: k for k, s in enumerate(slots)}

    tensor_count = lax.axis_size("tensor")
    cores = 2 - tensor_count % 2
    pod = (tensor_count // cores, cores)
    at = lax.axis_index("tensor")
    at_hi, at_lo = at // cores, at % cores

    pieces = []
    for i, j in slots:
        target = (me_hi + i) % grid[0] * grid[1] + (me_lo + j) % grid[1]
        piece = jnp.stack(
            [
                lax.dynamic_slice_in_dim(v, target * own_cols, own_cols, 1)
                for v in (tokens, tangent_in, cotangent)
            ]
        )
        pieces.append(shift(piece, grid, (i, j)))

    def from_chips(block):
        return jnp.stack([shift(block, pod, (i, 0), "tensor") for i in range(pod[0])], axis=2)

    def from_cores(held):
        both = jnp.stack([shift(held, pod, (0, k), "tensor") for k in range(pod[1])], axis=3)
        return both.reshape(-1, dp_count, tensor_count * own_rows, own_cols)

    (tok_cols,) = from_cores(from_chips(jnp.stack([p[:1] for p in pieces], axis=1)))
    later = from_chips(after(jnp.stack([p[1:] for p in pieces], axis=1), tok_cols))
    group_rows = tok_cols.shape[1]
    cut = group_rows // 2
    halves = [(0, slice(0, cut)), (1, slice(cut, group_rows))]

    def up(rows):
        return dot(rows, w_in)

    def back(rows):
        return lax.dot_general(
            rows, w_out, (((1,), (1,)), ((), ())), preferred_element_type=jnp.float32
        )

    def sums(terms):
        whole = [
            f(cols.reshape(dp_count * group_rows, own_cols)).reshape(dp_count, group_rows, -1)
            for f, cols in terms
        ]
        return [
            sum_to_owner(
                lambda s, r=rows: jnp.stack([w[place[s], r] for w in whole]),
                grid,
                first,
            )
            for first, rows in halves
        ]

    back_hi = (at_hi - jnp.arange(pod[0], dtype=jnp.int32)) % pod[0]
    back_lo = (at_lo - jnp.arange(pod[1], dtype=jnp.int32)) % pod[1]
    row_at = (
        (back_hi[:, None] * cores + back_lo[None, :])[:, :, None] * own_rows
        + jnp.arange(own_rows, dtype=jnp.int32)
    ).reshape(group_rows)
    keep = [(row_at[rows] < live_rows)[:, None] for _, rows in halves]

    def spread(values):
        values = [half(jnp.where(k, v, 0.0)) for k, v in zip(keep, values)]
        return [gather_first(v, grid, 1 - first) for v, (first, _) in zip(values, halves)]

    def everywhere(held):
        found = [gather_second(v, grid, 1 - first) for v, (first, _) in zip(held, halves)]
        return jnp.stack([jnp.concatenate([f[s] for f in found]) for s in slots])

    def down_cores(hidden):
        flat = hidden.reshape(dp_count * group_rows, -1)
        terms = dot(flat, w_out).reshape(dp_count, *pod, own_rows, own_cols)
        near = terms[:, :, 0]
        for k in range(1, pod[1]):
            near = near + shift(half(terms[:, :, k]), pod, (0, -k), "tensor").astype(jnp.float32)
        return near

    def down_chips(near):
        total = near[:, 0]
        for i in range(1, pod[0]):
            total = total + shift(half(near[:, i]), pod, (-i, 0), "tensor").astype(jnp.float32)
        return half(total)

    pre_act = [p[0] for p in sums([(up, tok_cols)])]
    pairs = [gelu_pair(p) for p in pre_act]
    act_held = spread([a for a, _ in pairs])
    later = from_cores(after(later, pre_act))
    tan_cols, cot_cols = after(later, act_held)
    act_all = everywhere(act_held)
    both = sums([(up, tan_cols), (back, cot_cols)])
    out_near = down_cores(act_all)
    both = after(both, out_near)
    dact_held = spread([s * v[0] for (_, s), v in zip(pairs, both)])
    dact_all = everywhere(dact_held)
    back_grad = after([v[1] for v in both], dact_held)
    grad_all = everywhere(spread([s * v for (_, s), v in zip(pairs, back_grad)]))
    summed = jnp.stack([down_chips(out_near), down_chips(down_cores(dact_all))], axis=1)
    cols = jnp.stack(
        [shift(summed[place[(i, j)]], grid, (-i, -j)) for i, j in slots]
    ).reshape(*grid, 2, own_rows, own_cols)
    cols = jnp.roll(jnp.roll(cols, me_hi, axis=0), me_lo, axis=1)
    out, tan = cols.transpose(2, 3, 0, 1, 4).reshape(2, own_rows, model_cols)
    grad_w_in = lax.dot_general(
        tok_cols.reshape(dp_count * group_rows, own_cols),
        grad_all.reshape(dp_count * group_rows, -1),
        (((0,), (0,)), ((), ())),
        preferred_element_type=jnp.float32,
    )
    return (out, tan, grad_w_in)


def solution(mesh):
    return jax.shard_map(
        local,
        mesh=mesh,
        in_specs=(
            P(("dp", "tensor"), None),
            P(("dp", "tensor"), None),
            P(("dp", "tensor"), None),
            P("dp", "tensor"),
            P("tensor", "dp"),
            P(),
            P(),
        ),
        out_specs=(P(("dp", "tensor"), None), P(("dp", "tensor"), None), P("dp", "tensor")),
        check_vma=False,
    )
```

```python
import math

import jax
import jax.numpy as jnp
from jax import lax
from jax.sharding import PartitionSpec as P

tanh_coef = math.sqrt(2.0 / math.pi)
cubic_coef = 0.044715


def gelu_pair(pre_act):
    inner_arg = tanh_coef * (pre_act + cubic_coef * pre_act * pre_act * pre_act)
    tanh_val = jnp.tanh(inner_arg)
    act_val = 0.5 * pre_act * (1.0 + tanh_val)
    slope_val = 0.5 * (1.0 + tanh_val) + 0.5 * pre_act * (1.0 - tanh_val * tanh_val) * tanh_coef * (
        1.0 + 3.0 * cubic_coef * pre_act * pre_act
    )
    return (act_val, slope_val)


def dot(a, b):
    return jnp.dot(a, b, preferred_element_type=jnp.float32)


def dp_grid(dp_count):
    lo = int(math.sqrt(dp_count))
    while dp_count % lo:
        lo -= 1
    return dp_count // lo, lo


def shift(value, grid, step, axis="dp"):
    hi, lo = grid
    if step[0] % hi == 0 and step[1] % lo == 0:
        return value
    pairs = [
        (a * lo + b, (a + step[0]) % hi * lo + (b + step[1]) % lo)
        for a in range(hi)
        for b in range(lo)
    ]
    return lax.ppermute(value, axis, pairs)


def after(value, *others):
    return lax.optimization_barrier((value, others))[0]


def axis_step(axis, size):
    return (size, 0) if axis == 0 else (0, size)


def half(value):
    return value.astype(jnp.bfloat16)


def sum_to_owner(part, grid, first):
    second = 1 - first
    n1, n2 = grid[first], grid[second]

    def slot(i, j):
        return (i, j) if first == 0 else (j, i)

    arrived = [
        shift(
            half(jnp.stack([part(slot(i, j)) for j in range(n2)])), grid, axis_step(first, -i)
        )
        for i in range(1, n1)
    ]
    sums = []
    for j in list(range(1, n2)) + [0]:
        total = part(slot(0, j))
        for piece in arrived:
            total = total + piece[j].astype(jnp.float32)
        sums.append(total if j == 0 else shift(half(total), grid, axis_step(second, -j)))
    total = sums[-1]
    for piece in sums[:-1]:
        total = total + piece.astype(jnp.float32)
    return total


def gather_first(value, grid, first):
    return jnp.stack([shift(value, grid, axis_step(first, i)) for i in range(grid[first])])


def gather_second(held, grid, first):
    second = 1 - first
    found = {}
    for j in range(grid[second]):
        there = shift(held, grid, axis_step(second, j))
        for i in range(grid[first]):
            found[(i, j) if first == 0 else (j, i)] = there[i]
    return found


def local(tokens, tangent_in, cotangent, w_in, w_out, clip_len, clip_dev):
    dp_count = lax.axis_size("dp")
    grid = dp_grid(dp_count)
    me = lax.axis_index("dp")
    me_hi, me_lo = me // grid[1], me % grid[1]
    live_rows = jnp.sum(jnp.where(clip_dev == me, clip_len, 0))
    own_rows, model_cols = tokens.shape
    own_cols = model_cols // dp_count
    slots = [(i, j) for i in range(grid[0]) for j in range(grid[1])]
    place = {s: k for k, s in enumerate(slots)}

    tensor_count = lax.axis_size("tensor")
    cores = 2 - tensor_count % 2
    pod = (tensor_count // cores, cores)
    at = lax.axis_index("tensor")
    at_hi, at_lo = at // cores, at % cores

    pieces = []
    for i, j in slots:
        target = (me_hi + i) % grid[0] * grid[1] + (me_lo + j) % grid[1]
        piece = jnp.stack(
            [
                lax.dynamic_slice_in_dim(v, target * own_cols, own_cols, 1)
                for v in (tokens, tangent_in, cotangent)
            ]
        )
        pieces.append(shift(piece, grid, (i, j)))

    def from_chips(block):
        return jnp.stack([shift(block, pod, (i, 0), "tensor") for i in range(pod[0])], axis=2)

    def from_cores(held):
        both = jnp.stack([shift(held, pod, (0, k), "tensor") for k in range(pod[1])], axis=3)
        return both.reshape(-1, dp_count, tensor_count * own_rows, own_cols)

    (tok_cols,) = from_cores(from_chips(jnp.stack([p[:1] for p in pieces], axis=1)))
    later = from_chips(after(jnp.stack([p[1:] for p in pieces], axis=1), tok_cols))
    group_rows = tok_cols.shape[1]
    cut = group_rows // 2
    halves = [(0, slice(0, cut)), (1, slice(cut, group_rows))]

    def up(rows):
        return dot(rows, w_in)

    def back(rows):
        return lax.dot_general(
            rows, w_out, (((1,), (1,)), ((), ())), preferred_element_type=jnp.float32
        )

    def sums(terms):
        return [
            sum_to_owner(
                lambda s, r=rows: jnp.stack([f(cols[place[s], r]) for f, cols in terms]),
                grid,
                first,
            )
            for first, rows in halves
        ]

    back_hi = (at_hi - jnp.arange(pod[0], dtype=jnp.int32)) % pod[0]
    back_lo = (at_lo - jnp.arange(pod[1], dtype=jnp.int32)) % pod[1]
    row_at = (
        (back_hi[:, None] * cores + back_lo[None, :])[:, :, None] * own_rows
        + jnp.arange(own_rows, dtype=jnp.int32)
    ).reshape(group_rows)
    keep = [(row_at[rows] < live_rows)[:, None] for _, rows in halves]

    def spread(values):
        values = [half(jnp.where(k, v, 0.0)) for k, v in zip(keep, values)]
        return [gather_first(v, grid, 1 - first) for v, (first, _) in zip(values, halves)]

    def everywhere(held):
        found = [gather_second(v, grid, 1 - first) for v, (first, _) in zip(held, halves)]
        return jnp.stack([jnp.concatenate([f[s] for f in found]) for s in slots])

    def down_cores(hidden):
        flat = hidden.reshape(dp_count * group_rows, -1)
        terms = dot(flat, w_out).reshape(dp_count, *pod, own_rows, own_cols)
        near = terms[:, :, 0]
        for k in range(1, pod[1]):
            near = near + shift(half(terms[:, :, k]), pod, (0, -k), "tensor").astype(jnp.float32)
        return near

    def down_chips(near):
        total = near[:, 0]
        for i in range(1, pod[0]):
            total = total + shift(half(near[:, i]), pod, (-i, 0), "tensor").astype(jnp.float32)
        return half(total)

    pre_act = [p[0] for p in sums([(up, tok_cols)])]
    pairs = [gelu_pair(p) for p in pre_act]
    act_held = spread([a for a, _ in pairs])
    later = from_cores(after(later, pre_act))
    tan_cols, cot_cols = after(later, act_held)
    act_all = everywhere(act_held)
    both = sums([(up, tan_cols), (back, cot_cols)])
    out_near = down_cores(act_all)
    both = after(both, out_near)
    dact_held = spread([s * v[0] for (_, s), v in zip(pairs, both)])
    dact_all = everywhere(dact_held)
    back_grad = [v[1] for v in both]
    grad_all = everywhere(spread([s * v for (_, s), v in zip(pairs, back_grad)]))
    summed = jnp.stack([down_chips(out_near), down_chips(down_cores(dact_all))], axis=1)
    cols = jnp.stack(
        [shift(summed[place[(i, j)]], grid, (-i, -j)) for i, j in slots]
    ).reshape(*grid, 2, own_rows, own_cols)
    cols = jnp.roll(jnp.roll(cols, me_hi, axis=0), me_lo, axis=1)
    out, tan = cols.transpose(2, 3, 0, 1, 4).reshape(2, own_rows, model_cols)
    grad_w_in = lax.dot_general(
        tok_cols.reshape(dp_count * group_rows, own_cols),
        grad_all.reshape(dp_count * group_rows, -1),
        (((0,), (0,)), ((), ())),
        preferred_element_type=jnp.float32,
    )
    return (out, tan, grad_w_in)


def solution(mesh):
    return jax.shard_map(
        local,
        mesh=mesh,
        in_specs=(
            P(("dp", "tensor"), None),
            P(("dp", "tensor"), None),
            P(("dp", "tensor"), None),
            P("dp", "tensor"),
            P("tensor", "dp"),
            P(),
            P(),
        ),
        out_specs=(P(("dp", "tensor"), None), P(("dp", "tensor"), None), P("dp", "tensor")),
        check_vma=False,
    )
```
